256 devices in a mesh: band: 32 (over z, y_hi, core), col: 8 (over x, y_lo).
Axes of the slice: x: 4, y: 4 (y_hi: 2, y_lo: 2; y = y_hi * 2 + y_lo), z: 8, core: 2. Of those that a mesh axis runs over, the one named last changes fastest.
Arguments:
- valence: bfloat16 [8, 64, 64, 128], P('col'), may hold values from -6 to 6
- conduction: bfloat16 [128, 64, 64, 128], P('band'), may hold values from -6 to 6
- energy_valence: float32 [8], P('col'), may hold values from -6 to -1
- energy_conduction: float32 [128], P('band'), may hold values from 0.5 to 6
- occ_valence: int32 [8], P('col'), may hold values from 1 to 2
- occ_conduction: int32 [128], P('band'), may hold values from 0 to 1
- gvec_index: int32 [10240], replicated, may hold values from 0 to 262143, as said below
Outputs:
- chi_zero: float32 [2, 10240, 10240], P(None, 'band', 'col')
The draws below stay inside these ranges and needn't reach their ends.
Inputs may be any that keep to these rules, and one draw needn't show every extreme that they name: `gvec_index`: distinct indices of the 10240 grid points with the shortest wave vectors, where index x * 64 * 64 + y * 64 + z stands for the vector with components ((x + 32) mod 64) - 32 and so on; ordered by length, equal lengths in any order.
All inputs are finite; a program needn't handle non-finite values.
Results may differ from the reference program's by a relative error of at most 0.01.
Values may be sent and summed in bfloat16 or wider, within the bound.
No kernel may reach another device: no remote copies, remote signals or barrier semaphores. Data moves between devices by JAX's collectives and lax.ppermute only.
A program may use at most 320 MiB of HBM per device.

```python
import math
import jax
import jax.numpy as jnp
from jax import lax

NG = 64
NPW = 10240
NV = 8
NC = 128


def draw_gvec_index(key, part):
    key = jax.random.fold_in(key, 11)
    total = NG * NG * NG
    flat = jnp.arange(total, dtype=jnp.int32)
    half = NG // 2
    comp_x = (flat // (NG * NG) + half) % NG - half
    comp_y = (flat // NG % NG + half) % NG - half
    comp_z = (flat % NG + half) % NG - half
    length = comp_x * comp_x + comp_y * comp_y + comp_z * comp_z
    tiebreak = jax.random.permutation(key, total).astype(jnp.int32)
    score = length * total + tiebreak
    order = jnp.argsort(score, stable=True).astype(jnp.int32)
    return order[:NPW]


def plant(array, key, least, high):
    spot = [jax.random.randint(jax.random.fold_in(key, axis), (), 0, length) for axis, length in enumerate(array.shape)]
    main_axis = array.shape.index(max(array.shape))
    neighbour = spot[:main_axis] + [(spot[main_axis] + 1) % array.shape[main_axis]] + spot[main_axis + 1:]
    return array.at[tuple(spot)].set(least).at[tuple(neighbour)].set(high)


def block_scale(own_key, shape, split, smallest, top_value):
    def one(dim, parts):
        draws = jax.random.uniform(jax.random.fold_in(jax.random.fold_in(own_key, 6), dim), (parts,), jnp.float32, smallest / len(split), top_value / len(split))
        return jnp.repeat(jnp.exp(draws), shape[dim] // parts).reshape((-1,) + (1,) * (len(shape) - dim - 1))

    gain = one(*split[0])
    for cut in split[1:]:
        gain = gain * one(*cut)
    return gain


def normal_values(stream_key, extent, scale, limit, split=(), kind=jnp.bfloat16):
    loudness = block_scale(stream_key, extent, split, -0.22, 0.18) if split else 1.0
    drawn = jax.random.normal(stream_key, extent, jnp.float32) * scale * loudness
    return jnp.minimum(jnp.maximum(drawn, -limit), limit).astype(kind)


def setup_inputs(seed: int = 0) -> dict:
    splits = jax.random.split(jax.random.key(seed), 8)
    return {
        "valence": normal_values(splits[0], (NV, NG, NG, 2 * NG), 1.0, 6.0, ((0, 8),)),
        "conduction": normal_values(splits[1], (NC, NG, NG, 2 * NG), 1.0, 6.0, ((0, 32),)),
        "energy_valence": jnp.clip(-6.0 + 5.0 * jax.random.uniform(splits[2], (NV,), jnp.float32) ** block_scale(splits[2], (NV,), ((0, 8),), -0.2, 0.2), -6.0, -1.0),
        "energy_conduction": jnp.clip(0.5 + 5.5 * jax.random.uniform(splits[3], (NC,), jnp.float32) ** block_scale(splits[3], (NC,), ((0, 32),), -0.2, 0.2), 0.5, 6.0),
        "occ_valence": plant(jax.random.randint(splits[4], (NV,), 1, 3), jax.random.fold_in(splits[4], 1), 1, 2).astype(jnp.int32),
        "occ_conduction": plant(jax.random.randint(splits[5], (NC,), 0, 2), jax.random.fold_in(splits[5], 1), 0, 1).astype(jnp.int32),
        "gvec_index": draw_gvec_index(jax.random.fold_in(splits[7], 71), 0),
    }


def dft_table():
    freq = jnp.arange(NG, dtype=jnp.int32)
    product = freq[:, None] * freq[None, :] % NG
    angle = 2.0 * math.pi / NG * product.astype(jnp.float32)
    cosine = jnp.cos(angle) / math.sqrt(NG)
    sine = jnp.sin(angle) / math.sqrt(NG)
    table = jnp.stack([jnp.stack([cosine, sine]), jnp.stack([-sine, cosine])])
    return table.astype(jnp.bfloat16)

def transform(field, table, form):
    return jnp.einsum(form, table.astype(jnp.float32), field.astype(jnp.float32)).astype(jnp.bfloat16)

def reference(valence, conduction, energy_valence, energy_conduction, occ_valence, occ_conduction, gvec_index):
    table = dft_table()
    val_grid = jnp.transpose(valence.reshape(NV, NG, NG, 2, NG), (0, 3, 1, 2, 4)).reshape(NV, 2, NG, NG * NG)
    val_re = val_grid[:, 0].astype(jnp.float32)
    val_im = val_grid[:, 1].astype(jnp.float32)

    def one_band(cond_band):
        cond_grid = jnp.transpose(cond_band.reshape(NG, NG, 2, NG), (2, 0, 1, 3)).reshape(2, NG, NG * NG)
        cond_re = cond_grid[0].astype(jnp.float32)
        cond_im = cond_grid[1].astype(jnp.float32)
        real_part = val_re * cond_re + val_im * cond_im
        imag_part = val_re * cond_im - val_im * cond_re
        field = jnp.stack([real_part, imag_part], axis=1).astype(jnp.bfloat16)
        field = field.reshape(NV, 2, NG, NG, NG)
        field = transform(field, table, 'oikx,vixyz->vokyz')
        field = transform(field, table, 'oiky,vixyz->voxkz')
        field = transform(field, table, 'oikz,vixyz->voxyk')
        flat = field.reshape(NV, 2, NG * NG * NG)
        return jnp.take(flat, gvec_index, axis=2)
    rho = lax.map(one_band, conduction)
    rho = jnp.transpose(rho, (1, 0, 2, 3))
    count = conduction.shape[0]
    occ_diff = (occ_valence[:, None] - occ_conduction[None, :]).astype(jnp.float32)
    weight = occ_diff / (energy_valence[:, None] - energy_conduction[None, :]) / math.sqrt(NV * count)
    weighted = (weight[:, :, None, None] * rho.astype(jnp.float32)).astype(jnp.bfloat16)
    rotated = jnp.stack([-rho[:, :, 1], rho[:, :, 0]], axis=2)
    columns = jnp.concatenate([rho, rotated], axis=3)
    tile = lax.dot_general(weighted.astype(jnp.float32), columns.astype(jnp.float32), (((0, 1, 2), (0, 1, 2)), ((), ())), preferred_element_type=jnp.float32)
    npw = rho.shape[3]
    return jnp.transpose(tile.reshape(npw, 2, npw), (1, 0, 2))
```

```python
import functools
import math

import jax
import jax.numpy as jnp
import numpy as np
from jax import lax
from jax.experimental import pallas as pl
from jax.experimental.pallas import tpu as pltpu
from jax.sharding import PartitionSpec as P
from ml_dtypes import bfloat16

NG = 64
NPW = 10240


def sphere_radius():
    axis = (np.arange(NG) + NG // 2) % NG - NG // 2
    square = axis * axis
    length = np.sort((square[:, None, None] + square[None, :, None] + square[None, None, :]).ravel())
    return int(length[NPW - 1])


LIMIT = sphere_radius()
KMAX = math.isqrt(LIMIT)
KS = list(range(-KMAX, KMAX + 1))
NK = len(KS)
YORDER = [0]
for step in range(1, KMAX + 1):
    YORDER += [step, -step]
NY = -(-len(YORDER) // 8) * 8
YORDER += [0] * (NY - len(YORDER))


def rows_for(kx):
    return -(-(2 * math.isqrt(LIMIT - kx * kx) + 1) // 8) * 8


BASE = []
total = 0
for kx in KS:
    BASE.append(total)
    total += rows_for(kx)
USED_ROWS = total
ROWS = -(-total // 256) * 256


def cos_sin(freqs):
    product = np.asarray(freqs)[:, None] * np.arange(NG)[None, :] % NG
    angle = (2.0 * math.pi / NG) * product
    scale = 1.0 / math.sqrt(NG)
    return np.cos(angle) * scale, np.sin(angle) * scale


def x_matrix():
    cos, sin = cos_sin(KS)
    eye = np.eye(8)
    return np.concatenate([np.kron(cos, eye), np.kron(sin, eye)], axis=0).astype(bfloat16)


def y_matrix():
    cos, sin = cos_sin(YORDER)
    return np.concatenate([cos, sin], axis=0).astype(bfloat16)


def z_matrix(pairs):
    cos, sin = cos_sin(KS)
    out = np.zeros((NK, 2, pairs, pairs, 2, NG), np.float64)
    for p in range(pairs):
        out[:, 0, p, p, 0] = cos
        out[:, 0, p, p, 1] = sin
        out[:, 1, p, p, 0] = -sin
        out[:, 1, p, p, 1] = cos
    return out.reshape(NK * 2 * pairs, pairs * 2 * NG).astype(bfloat16)


def signed(index):
    return ((index + NG // 2) & (NG - 1)) - NG // 2


def density_kernel(
    pairs, dests, col_width, row_width,
    v_ref, c_ref, xm_ref, ym_ref, zm_ref, g_ref, ev_ref, ec_ref, ov_ref, oc_ref,
    rho_ref, row_ref,
    first_ref, second_ref, pos_ref, kz_ref, flat_ref,
):
    step = pl.program_id(0)
    lanes = pairs * 2 * NG
    lane = lax.broadcasted_iota(jnp.int32, (1, 1, 2 * NG), 2)
    low = lane < NG
    field_v = v_ref[0].astype(jnp.float32)
    turned = pltpu.roll(field_v, NG, 2)
    v_re = jnp.where(low, field_v, turned)
    v_im = jnp.where(low, turned, -field_v)
    parts = []
    for p in range(pairs):
        field_c = c_ref[p].astype(jnp.float32)
        parts.append(v_re * field_c + v_im * pltpu.roll(field_c, NG, 2))
    sign = jnp.where(lax.broadcasted_iota(jnp.int32, (1, 2 * NG), 1) < NG, 1.0, -1.0)

    def combine(both, rows):
        cols = []
        for p in range(pairs):
            take = slice(p * 2 * NG, (p + 1) * 2 * NG)
            cols.append(both[:rows, take] + sign * pltpu.roll(both[rows : 2 * rows, take], NG, 1))
        return jnp.concatenate(cols, axis=1)

    halves = []
    for half in range(2):
        stacked = jnp.concatenate(
            [
                part[:, half * 8 : half * 8 + 8].reshape(NG * 8, 2 * NG).astype(jnp.bfloat16)
                for part in parts
            ],
            axis=1,
        )
        both = jnp.dot(xm_ref[...], stacked, preferred_element_type=jnp.float32)
        halves.append(combine(both, NK * 8).reshape(NK, 8, lanes))
    merged = jnp.concatenate(halves, axis=1).astype(jnp.bfloat16)
    first_ref[:, pl.ds(pl.multiple_of(step * 16, 16), 16), :] = merged

    @pl.when(step == pl.num_programs(0) - 1)
    def _():
        second_ref[USED_ROWS:, :] = jnp.zeros((ROWS - USED_ROWS, lanes), jnp.float32)
        for i, kx in enumerate(KS):
            both = jnp.dot(ym_ref[...], first_ref[i], preferred_element_type=jnp.float32)
            second_ref[BASE[i] : BASE[i] + rows_for(kx), :] = combine(both, NY)[: rows_for(kx)]
        second = second_ref[...].astype(jnp.bfloat16)
        third = lax.dot_general(
            zm_ref[...], second, (((1,), (1,)), ((), ())), preferred_element_type=jnp.float32
        ).astype(jnp.bfloat16)
        index = g_ref[...]
        comp_x = signed(index >> 12)
        comp_y = signed((index >> 6) & (NG - 1))
        place = 2 * jnp.abs(comp_y) - (comp_y > 0).astype(jnp.int32)
        for i, kx in enumerate(KS):
            place = jnp.where(comp_x == kx, place + BASE[i], place)
        pos_ref[...] = place
        kz_ref[...] = signed(index & (NG - 1)) + KMAX
        row_id = lax.broadcasted_iota(jnp.int32, (ROWS, 256), 0)
        blocks = col_width // 256

        def body(dest, carry):
            for k in range(blocks):
                which = dest * blocks + k
                pos = pos_ref[pl.ds(which, 1), :]
                kz = kz_ref[pl.ds(which, 1), :]
                pick = jnp.where(row_id == pos, 1.0, 0.0).astype(jnp.bfloat16)
                found = jnp.dot(third, pick, preferred_element_type=jnp.float32)
                found = found.reshape(NK, 2 * pairs, 256)
                acc = jnp.zeros((2 * pairs, 256), jnp.float32)
                for i in range(NK):
                    acc = jnp.where(kz == i, found[i], acc)
                rho_ref[dest, :, k * 256 : (k + 1) * 256] = acc.astype(jnp.bfloat16)
                flat_ref[which] = acc
            return carry

        lax.fori_loop(0, dests, body, 0)
        which_pair = lax.broadcasted_iota(jnp.int32, (2 * pairs, 128), 0) % pairs
        occ_diff = jnp.zeros((2 * pairs, 128), jnp.float32)
        energy = jnp.ones((2 * pairs, 128), jnp.float32)
        for p in range(pairs):
            occ_diff = jnp.where(which_pair == p, (ov_ref[0] - oc_ref[p]).astype(jnp.float32), occ_diff)
            energy = jnp.where(which_pair == p, ev_ref[0] - ec_ref[p], energy)
        weight = (occ_diff / energy / math.sqrt(1024))[:, :1]
        group = math.lcm(row_width, 256)

        def row_body(block, carry):
            wide = jnp.concatenate(
                [flat_ref[block * (group // 256) + k] for k in range(group // 256)], axis=1
            )
            wide = (wide * weight).astype(jnp.bfloat16).astype(jnp.float32)
            for k in range(group // row_width):
                row_ref[block * (group // row_width) + k] = wide[
                    :, k * row_width : (k + 1) * row_width
                ].astype(jnp.bfloat16)
            return carry

        lax.fori_loop(0, NPW // group, row_body, 0)


def densities(valence, conduction, energy_valence, energy_conduction, occ_valence, occ_conduction, gvec_index, n_col, n_band):
    pairs = conduction.shape[0]
    lanes = pairs * 2 * NG
    col_width = NPW // n_col
    row_width = NPW // n_band
    smem = pl.BlockSpec(memory_space=pltpu.SMEM)
    whole = lambda shape: pl.BlockSpec(shape, lambda s: (0,) * len(shape))
    xm, ym, zm = x_matrix(), y_matrix(), z_matrix(pairs)
    return pl.pallas_call(
        functools.partial(density_kernel, pairs, n_col, col_width, row_width),
        grid=(NG // 16,),
        in_specs=[
            pl.BlockSpec((1, NG, 16, 2 * NG), lambda s: (0, 0, s, 0)),
            pl.BlockSpec((pairs, NG, 16, 2 * NG), lambda s: (0, 0, s, 0)),
            whole(xm.shape), whole(ym.shape), whole(zm.shape),
            whole((NPW // 256, 256)),
            smem, smem, smem, smem,
        ],
        out_specs=[whole((n_col, 2 * pairs, col_width)), whole((n_band, 2 * pairs, row_width))],
        out_shape=[
            jax.ShapeDtypeStruct((n_col, 2 * pairs, col_width), jnp.bfloat16),
            jax.ShapeDtypeStruct((n_band, 2 * pairs, row_width), jnp.bfloat16),
        ],
        scratch_shapes=[
            pltpu.VMEM((NK, NG, lanes), jnp.bfloat16),
            pltpu.VMEM((ROWS, lanes), jnp.float32),
            pltpu.VMEM((NPW // 256, 256), jnp.int32),
            pltpu.VMEM((NPW // 256, 256), jnp.int32),
            pltpu.VMEM((NPW // 256, 2 * pairs, 256), jnp.float32),
        ],
        compiler_params=pltpu.CompilerParams(vmem_limit_bytes=48 * 1024 * 1024),
        cost_estimate=pl.CostEstimate(flops=2 * 10**9, bytes_accessed=6 * 10**6, transcendentals=0),
    )(
        valence, conduction, jnp.asarray(xm), jnp.asarray(ym), jnp.asarray(zm),
        gvec_index.reshape(NPW // 256, 256),
        energy_valence, energy_conduction, occ_valence, occ_conduction,
    )


def contract_kernel(n_bands, r_ref, c_ref, out_ref, lhs_ref):
    step = pl.program_id(0)
    width = r_ref.shape[-1]

    @pl.when(step == 0)
    def _():
        rows = r_ref[...]
        nv, nb, po, _ = rows.shape
        f = rows.astype(jnp.float32)
        half = po // 2
        swapped = jnp.concatenate([f[:, :, half:], -f[:, :, :half]], axis=2)
        for v in range(nv):
            for src, which in ((f, 0), (swapped, 1)):
                lhs_ref[v, which * width : (which + 1) * width, :] = (
                    src[v].reshape(nb * po, width).T.astype(jnp.bfloat16)
                )

    tile = c_ref.shape[-1]
    nv = lhs_ref.shape[0]
    nb, _, po, _ = c_ref.shape
    acc = jnp.zeros((2 * width, tile), jnp.float32)
    for v in range(nv):
        cols = c_ref[:, v].astype(jnp.float32).reshape(nb * po, tile).astype(jnp.bfloat16)
        acc += jnp.dot(lhs_ref[v], cols, preferred_element_type=jnp.float32)
    out_ref[...] = acc.reshape(2, width, tile)


def contract(rows, cols):
    nv, nb, po, width = rows.shape
    total = cols.shape[-1]
    tile = 256
    return pl.pallas_call(
        functools.partial(contract_kernel, nb),
        grid=(total // tile,),
        in_specs=[
            pl.BlockSpec(rows.shape, lambda s: (0, 0, 0, 0)),
            pl.BlockSpec((nb, nv, po, tile), lambda s: (0, 0, 0, s)),
        ],
        out_specs=pl.BlockSpec((2, width, tile), lambda s: (0, 0, s)),
        out_shape=jax.ShapeDtypeStruct((2, width, total), jnp.float32),
        scratch_shapes=[pltpu.VMEM((nv, 2 * width, nb * po), jnp.bfloat16)],
        compiler_params=pltpu.CompilerParams(vmem_limit_bytes=48 * 1024 * 1024),
        cost_estimate=pl.CostEstimate(
            flops=4 * nv * nb * po * width * total, bytes_accessed=10**7, transcendentals=0
        ),
    )(rows, cols)


def local(
    valence, conduction, energy_valence, energy_conduction, occ_valence, occ_conduction, gvec_index
):
    n_col, n_band = lax.axis_size("col"), lax.axis_size("band")
    pairs = conduction.shape[0]
    rho, weighted = densities(
        valence, conduction, energy_valence, energy_conduction, occ_valence, occ_conduction,
        gvec_index, n_col, n_band,
    )
    cols = lax.all_to_all(rho, "col", split_axis=0, concat_axis=0, tiled=True)
    rows = lax.all_to_all(weighted, "band", split_axis=0, concat_axis=0, tiled=True)
    cols = lax.all_gather(cols, "band", axis=0)
    rows = lax.all_gather(rows, "col", axis=0)
    return contract(rows, cols)


def solution(mesh):
    return jax.shard_map(
        local,
        mesh=mesh,
        in_specs=(
            P("col", None, None, None),
            P("band", None, None, None),
            P("col"),
            P("band"),
            P("col"),
            P("band"),
            P(),
        ),
        out_specs=P(None, "band", "col"),
        check_vma=False,
    )
```

```python
import functools
import math

import jax
import jax.numpy as jnp
import numpy as np
from jax import lax
from jax.experimental import pallas as pl
from jax.experimental.pallas import tpu as pltpu
from jax.sharding import PartitionSpec as P
from ml_dtypes import bfloat16

NG = 64
NPW = 10240
QUAD = 4
TILE = 256
VMEM_LIMIT = 60 * 1024 * 1024
SMALL_LIMIT = 16 * 1024 * 1024


def sphere_radius():
    axis = (np.arange(NG) + NG // 2) % NG - NG // 2
    square = axis * axis
    length = np.sort((square[:, None, None] + square[None, :, None] + square[None, None, :]).ravel())
    return int(length[NPW - 1])


LIMIT = sphere_radius()
KMAX = math.isqrt(LIMIT)
KS = list(range(-KMAX, KMAX + 1))
NK = len(KS)
YORDER = [0]
for step in range(1, KMAX + 1):
    YORDER += [step, -step]
NY = -(-len(YORDER) // 8) * 8
YORDER += [0] * (NY - len(YORDER))


def rows_for(kx):
    return -(-(2 * math.isqrt(LIMIT - kx * kx) + 1) // 8) * 8


BASE = []
total = 0
for kx in KS:
    BASE.append(total)
    total += rows_for(kx)
USED_ROWS = total
ROWS = -(-total // 256) * 256


def cos_sin(freqs):
    product = np.asarray(freqs)[:, None] * np.arange(NG)[None, :] % NG
    angle = (2.0 * math.pi / NG) * product
    scale = 1.0 / math.sqrt(NG)
    return np.cos(angle) * scale, np.sin(angle) * scale


def x_matrix():
    cos, sin = cos_sin(KS)
    eye = np.eye(8)
    return np.concatenate([np.kron(cos, eye), np.kron(sin, eye)], axis=0).astype(bfloat16)


def y_matrix():
    cos, sin = cos_sin(YORDER)
    return np.concatenate([cos, sin], axis=0).astype(bfloat16)


def z_matrix(pairs):
    cos, sin = cos_sin(KS)
    out = np.zeros((NK, 2, pairs, pairs, 2, NG), np.float64)
    for p in range(pairs):
        out[:, 0, p, p, 0] = cos
        out[:, 0, p, p, 1] = sin
        out[:, 1, p, p, 0] = -sin
        out[:, 1, p, p, 1] = cos
    return out.reshape(NK * 2 * pairs, pairs * 2 * NG).astype(bfloat16)


def signed(index):
    return ((index + NG // 2) & (NG - 1)) - NG // 2


def density_kernel(
    pairs, dests, col_width,
    v_ref, c_ref, xm_ref, ym_ref, zm_ref, g_ref, ev_ref, ec_ref, ov_ref, oc_ref,
    rho_ref, weighted_ref,
    first_ref, second_ref, pos_ref, kz_ref, flat_ref,
):
    step = pl.program_id(0)
    lanes = pairs * 2 * NG
    lane = lax.broadcasted_iota(jnp.int32, (1, 1, 2 * NG), 2)
    low = lane < NG
    field_v = v_ref[0].astype(jnp.float32)
    turned = pltpu.roll(field_v, NG, 2)
    v_re = jnp.where(low, field_v, turned)
    v_im = jnp.where(low, turned, -field_v)
    parts = []
    for p in range(pairs):
        field_c = c_ref[p].astype(jnp.float32)
        parts.append(v_re * field_c + v_im * pltpu.roll(field_c, NG, 2))
    sign = jnp.where(lax.broadcasted_iota(jnp.int32, (1, 2 * NG), 1) < NG, 1.0, -1.0)

    def combine(both, rows):
        cols = []
        for p in range(pairs):
            take = slice(p * 2 * NG, (p + 1) * 2 * NG)
            cols.append(both[:rows, take] + sign * pltpu.roll(both[rows : 2 * rows, take], NG, 1))
        return jnp.concatenate(cols, axis=1)

    halves = []
    for half in range(2):
        stacked = jnp.concatenate(
            [
                part[:, half * 8 : half * 8 + 8].reshape(NG * 8, 2 * NG).astype(jnp.bfloat16)
                for part in parts
            ],
            axis=1,
        )
        both = jnp.dot(xm_ref[...], stacked, preferred_element_type=jnp.float32)
        halves.append(combine(both, NK * 8).reshape(NK, 8, lanes))
    merged = jnp.concatenate(halves, axis=1).astype(jnp.bfloat16)
    first_ref[:, pl.ds(pl.multiple_of(step * 16, 16), 16), :] = merged

    @pl.when(step == pl.num_programs(0) - 1)
    def _():
        second_ref[USED_ROWS:, :] = jnp.zeros((ROWS - USED_ROWS, lanes), jnp.float32)
        for i, kx in enumerate(KS):
            both = jnp.dot(ym_ref[...], first_ref[i], preferred_element_type=jnp.float32)
            second_ref[BASE[i] : BASE[i] + rows_for(kx), :] = combine(both, NY)[: rows_for(kx)]
        second = second_ref[...].astype(jnp.bfloat16)
        third = lax.dot_general(
            zm_ref[...], second, (((1,), (1,)), ((), ())), preferred_element_type=jnp.float32
        ).astype(jnp.bfloat16)
        index = g_ref[...]
        comp_x = signed(index >> 12)
        comp_y = signed((index >> 6) & (NG - 1))
        place = 2 * jnp.abs(comp_y) - (comp_y > 0).astype(jnp.int32)
        for i, kx in enumerate(KS):
            place = jnp.where(comp_x == kx, place + BASE[i], place)
        pos_ref[...] = place
        kz_ref[...] = signed(index & (NG - 1)) + KMAX
        row_id = lax.broadcasted_iota(jnp.int32, (ROWS, 256), 0)
        blocks = col_width // 256

        def body(dest, carry):
            for k in range(blocks):
                which = dest * blocks + k
                pos = pos_ref[pl.ds(which, 1), :]
                kz = kz_ref[pl.ds(which, 1), :]
                pick = jnp.where(row_id == pos, 1.0, 0.0).astype(jnp.bfloat16)
                found = jnp.dot(third, pick, preferred_element_type=jnp.float32)
                found = found.reshape(NK, 2 * pairs, 256)
                acc = jnp.zeros((2 * pairs, 256), jnp.float32)
                for i in range(NK):
                    acc = jnp.where(kz == i, found[i], acc)
                rho_ref[dest, :, k * 256 : (k + 1) * 256] = acc.astype(jnp.bfloat16)
                flat_ref[which] = acc
            return carry

        lax.fori_loop(0, dests, body, 0)
        which_pair = lax.broadcasted_iota(jnp.int32, (2 * pairs, 128), 0) % pairs
        occ_diff = jnp.zeros((2 * pairs, 128), jnp.float32)
        energy = jnp.ones((2 * pairs, 128), jnp.float32)
        for p in range(pairs):
            occ_diff = jnp.where(which_pair == p, (ov_ref[0] - oc_ref[p]).astype(jnp.float32), occ_diff)
            energy = jnp.where(which_pair == p, ev_ref[0] - ec_ref[p], energy)
        weight = (occ_diff / energy / math.sqrt(1024))[:, :1]

        def weigh(dest, carry):
            for k in range(blocks):
                wide = flat_ref[dest * blocks + k] * weight
                weighted_ref[dest, :, k * 256 : (k + 1) * 256] = wide.astype(jnp.bfloat16)
            return carry

        lax.fori_loop(0, dests, weigh, 0)


def densities(valence, conduction, energy_valence, energy_conduction, occ_valence, occ_conduction, gvec_index, n_col):
    pairs = conduction.shape[0]
    lanes = pairs * 2 * NG
    col_width = NPW // n_col
    smem = pl.BlockSpec(memory_space=pltpu.SMEM)
    whole = lambda shape: pl.BlockSpec(shape, lambda s: (0,) * len(shape))
    xm, ym, zm = x_matrix(), y_matrix(), z_matrix(pairs)
    return pl.pallas_call(
        functools.partial(density_kernel, pairs, n_col, col_width),
        grid=(NG // 16,),
        in_specs=[
            pl.BlockSpec((1, NG, 16, 2 * NG), lambda s: (0, 0, s, 0)),
            pl.BlockSpec((pairs, NG, 16, 2 * NG), lambda s: (0, 0, s, 0)),
            whole(xm.shape), whole(ym.shape), whole(zm.shape),
            whole((NPW // 256, 256)),
            smem, smem, smem, smem,
        ],
        out_specs=[whole((n_col, 2 * pairs, col_width))] * 2,
        out_shape=[jax.ShapeDtypeStruct((n_col, 2 * pairs, col_width), jnp.bfloat16)] * 2,
        scratch_shapes=[
            pltpu.VMEM((NK, NG, lanes), jnp.bfloat16),
            pltpu.VMEM((ROWS, lanes), jnp.float32),
            pltpu.VMEM((NPW // 256, 256), jnp.int32),
            pltpu.VMEM((NPW // 256, 256), jnp.int32),
            pltpu.VMEM((NPW // 256, 2 * pairs, 256), jnp.float32),
        ],
        compiler_params=pltpu.CompilerParams(vmem_limit_bytes=VMEM_LIMIT),
        cost_estimate=pl.CostEstimate(flops=2 * 10**9, bytes_accessed=6 * 10**6, transcendentals=0),
    )(
        valence, conduction, jnp.asarray(xm), jnp.asarray(ym), jnp.asarray(zm),
        gvec_index.reshape(NPW // 256, 256),
        energy_valence, energy_conduction, occ_valence, occ_conduction,
    )


def split_kernel(x_ref, out0_ref, out1_ref, out2_ref, out3_ref, hold_ref):
    me = lax.axis_index("band") % QUAD
    width = out0_ref.shape[-1]
    for k in range(QUAD):
        hold_ref[k] = x_ref[:, k * width : (k + 1) * width]
    for k, ref in enumerate((out0_ref, out1_ref, out2_ref, out3_ref)):
        ref[...] = hold_ref[me ^ k]


def split(x):
    rows, total = x.shape
    return pl.pallas_call(
        split_kernel,
        out_shape=[jax.ShapeDtypeStruct((rows, total // QUAD), jnp.bfloat16)] * QUAD,
        scratch_shapes=[pltpu.VMEM((QUAD, rows, total // QUAD), jnp.bfloat16)],
        compiler_params=pltpu.CompilerParams(vmem_limit_bytes=SMALL_LIMIT),
    )(x)


def stack_kernel(*refs):
    for k, ref in enumerate(refs[:-2]):
        refs[-1][k] = ref[...]


def stack(parts, after):
    vmem = pl.BlockSpec(memory_space=pltpu.VMEM)
    return pl.pallas_call(
        stack_kernel,
        in_specs=[vmem] * len(parts) + [pl.BlockSpec(memory_space=pl.ANY)],
        out_specs=vmem,
        out_shape=jax.ShapeDtypeStruct((len(parts),) + parts[0].shape, jnp.bfloat16),
        compiler_params=pltpu.CompilerParams(vmem_limit_bytes=SMALL_LIMIT),
    )(*parts, after)


def left_kernel(n_col, depth, own_ref, next_ref, prev_ref, high_ref, low_ref, out_ref, hold_ref):
    col = lax.axis_index("col")
    plane = lax.axis_index("band") // QUAD
    xs = n_col // 2
    x, y = col // 2, col % 2

    def put(source, ref):
        hold_ref[source] = ref[...].astype(jnp.float32)

    for k in range(2):
        put(x * 2 + (y ^ k), own_ref.at[k])
        put((x + xs - 1) % xs * 2 + (y ^ k), next_ref.at[k])
        put((x + 1) % xs * 2 + (y ^ k), prev_ref.at[k])
    put((x + 2) % xs * 2 + y, high_ref)
    put((x + 2) % xs * 2 + (y ^ 1), low_ref)
    n, quad, rows, width = hold_ref.shape
    po = rows // depth
    turns = [0]
    for step in range(1, depth // 2):
        turns += [step, depth - step]
    turns.append(depth // 2)
    depth_rows = quad * n * po
    for slot, turn in enumerate(turns):
        source = pl.multiple_of((plane + depth - turn) % depth * po, po)
        f = hold_ref[:, :, pl.ds(source, po), :]
        f = jnp.concatenate([f[:, k] for k in range(quad)], axis=0)
        swapped = jnp.concatenate([f[:, po // 2 :], -f[:, : po // 2]], axis=1)
        for which, src in enumerate((f, swapped)):
            out_ref[which * width : (which + 1) * width, slot * depth_rows : (slot + 1) * depth_rows] = (
                src.reshape(depth_rows, width).astype(jnp.bfloat16).T
            )


def left(n_col, depth, parts):
    _, quad, rows, width = parts[0].shape
    return pl.pallas_call(
        functools.partial(left_kernel, n_col, depth),
        out_shape=jax.ShapeDtypeStruct((2 * width, depth * quad * rows), jnp.bfloat16),
        scratch_shapes=[pltpu.VMEM((n_col, quad, rows, width), jnp.float32)],
        compiler_params=pltpu.CompilerParams(vmem_limit_bytes=SMALL_LIMIT),
    )(*parts)


def product_on(core, turns, l_ref, blocks, out_ref, out_buf, sem):
    double = l_ref.shape[0]
    total = out_ref.shape[-1]
    slots = len(turns)
    quarter = l_ref.shape[1] // slots // QUAD
    copies = []
    for t in range(total // TILE):
        take = slice(t * TILE, (t + 1) * TILE)
        pieces = [None] * (slots * QUAD)
        at = 0
        for step, mirrored, count in turns:
            if step == 0:
                slot = 0
            elif 2 * step == slots:
                slot = slots - 1
            else:
                slot = 2 * step - 1 if core == mirrored else 2 * step
            each = QUAD // count
            for part in range(count):
                for k in range(each):
                    pieces[slot * QUAD + part * each + (k ^ mirrored)] = blocks[at + part][
                        k * quarter : (k + 1) * quarter, take
                    ]
            at += count
        tile = jnp.dot(
            l_ref[...], jnp.concatenate(pieces, axis=0), preferred_element_type=jnp.float32
        )
        out_buf[:, :, take] = tile.reshape(2, double // 2, TILE)
        copy = pltpu.make_async_copy(out_buf.at[:, :, take], out_ref.at[:, :, take], sem.at[t])
        copy.start()
        copies.append(copy)
    for copy in copies:
        copy.wait()


def product_kernel(turns, l_ref, *refs):
    out_ref, out_buf, sem = refs[-3:]
    core = lax.axis_index("band") % 2
    for which in range(2):
        pl.when(core == which)(
            functools.partial(
                product_on, which, turns, l_ref, refs[:-3], out_ref, out_buf, sem
            )
        )


def product(lhs, groups):
    double, all_rows = lhs.shape
    blocks = [b for g in groups for b in g[2]]
    total = blocks[0].shape[1]
    vmem = pl.BlockSpec(memory_space=pltpu.VMEM)
    return pl.pallas_call(
        functools.partial(product_kernel, [g[:2] + (len(g[2]),) for g in groups]),
        in_specs=[vmem] * (1 + len(blocks)),
        out_specs=pl.BlockSpec(memory_space=pl.ANY),
        out_shape=jax.ShapeDtypeStruct((2, double // 2, total), jnp.float32),
        scratch_shapes=[
            pltpu.VMEM((2, double // 2, total), jnp.float32),
            pltpu.SemaphoreType.DMA((total // TILE,)),
        ],
        compiler_params=pltpu.CompilerParams(vmem_limit_bytes=SMALL_LIMIT),
    )(lhs, *blocks)


def permute(x, n_band, n_col, move):
    pairs = []
    for band in range(n_band):
        for col in range(n_col):
            to_band, to_col = move(band, col)
            pairs.append((band * n_col + col, to_band * n_col + to_col))
    return lax.ppermute(x, ("band", "col"), pairs)


def local(
    valence, conduction, energy_valence, energy_conduction, occ_valence, occ_conduction, gvec_index
):
    n_col, n_band = lax.axis_size("col"), lax.axis_size("band")
    depth = n_band // QUAD
    xs = n_col // 2
    send = functools.partial(permute, n_band=n_band, n_col=n_col)
    shift = lambda band, by: (band // QUAD + by) % depth * QUAD + band % QUAD
    ring = lambda x: send(x, move=lambda b, c: (shift(b, 1 if b % 2 == 0 else -1), c))
    swap = lambda x: send(x, move=lambda b, c: (b ^ 1, c))
    high = lambda x: send(x, move=lambda b, c: (b ^ 2, c))
    along_x = lambda x, by: send(x, move=lambda b, c: (b, (c // 2 + by) % xs * 2 + c % 2))
    rho, weighted = densities(
        valence, conduction, energy_valence, energy_conduction, occ_valence, occ_conduction,
        gvec_index, n_col,
    )
    lines = [[z * QUAD + q for z in range(depth)] for q in range(QUAD)]
    weighted = lax.all_to_all(
        weighted, "band", split_axis=0, concat_axis=0, tiled=True, axis_index_groups=lines
    )
    own = lax.all_to_all(rho, "col", split_axis=0, concat_axis=0, tiled=True)
    size = own.shape[0] * own.shape[1]
    own = own.reshape(size, own.shape[2])
    weighted = weighted.reshape(size, weighted.shape[2])

    across = high(own)
    near_ring = [jnp.concatenate([own, swap(own)], axis=0)]
    near_ring.append(ring(near_ring[0]))
    parts = split(weighted)
    parts = [parts[0]] + [
        send(parts[k], move=lambda b, c, k=k: (b ^ k, c)) for k in range(1, QUAD)
    ]
    far_ring = [jnp.concatenate([across, swap(across)], axis=0)]
    far_ring.append(ring(far_ring[0]))
    near_ring.append(ring(near_ring[1]))
    mine = stack(parts, near_ring[2])
    beside = send(mine, move=lambda b, c: (b, c ^ 1))
    far_ring.append(ring(far_ring[1]))
    near_ring.append(ring(near_ring[2]))
    pair = stack([mine, beside], near_ring[3])
    after, before = along_x(pair, 1), along_x(pair, -1)
    far_ring.append(ring(far_ring[2]))
    last = [ring(near_ring[-1][:size]), ring(far_ring[-1][:size])]
    parts = [pair, after, before, along_x(after[0], 1), along_x(before[1], -1)]
    groups = [(0, 0, (near_ring[0], far_ring[0]))]
    for step in range(1, depth // 2):
        groups.append((step, 0, (near_ring[step], far_ring[step])))
        groups.append((step, 1, (swap(near_ring[step]), swap(far_ring[step]))))
    groups.append((depth // 2, 0, (last[0], swap(last[0]), last[1], swap(last[1]))))
    return product(left(n_col, depth, parts), groups)


def solution(mesh):
    return jax.shard_map(
        local,
        mesh=mesh,
        in_specs=(
            P("col", None, None, None),
            P("band", None, None, None),
            P("col"),
            P("band"),
            P("col"),
            P("band"),
            P(),
        ),
        out_specs=P(None, "band", "col"),
        check_vma=False,
    )
```

```python
import functools
import math

import jax
import jax.numpy as jnp
import numpy as np
from jax import lax
from jax.experimental import pallas as pl
from jax.experimental.pallas import tpu as pltpu
from jax.sharding import PartitionSpec as P
from ml_dtypes import bfloat16

NG = 64
NPW = 10240
QUAD = 4
TILE = 256
VMEM_LIMIT = 56 * 1024 * 1024
SMALL_LIMIT = 8 * 1024 * 1024


def sphere_radius():
    axis = (np.arange(NG) + NG // 2) % NG - NG // 2
    square = axis * axis
    length = np.sort((square[:, None, None] + square[None, :, None] + square[None, None, :]).ravel())
    return int(length[NPW - 1])


LIMIT = sphere_radius()
KMAX = math.isqrt(LIMIT)
KS = list(range(-KMAX, KMAX + 1))
NK = len(KS)
YORDER = [0]
for step in range(1, KMAX + 1):
    YORDER += [step, -step]
NY = -(-len(YORDER) // 8) * 8
YORDER += [0] * (NY - len(YORDER))


def rows_for(kx):
    return -(-(2 * math.isqrt(LIMIT - kx * kx) + 1) // 8) * 8


BASE = []
total = 0
for kx in KS:
    BASE.append(total)
    total += rows_for(kx)
USED_ROWS = total
ROWS = -(-total // 256) * 256


def cos_sin(freqs):
    product = np.asarray(freqs)[:, None] * np.arange(NG)[None, :] % NG
    angle = (2.0 * math.pi / NG) * product
    scale = 1.0 / math.sqrt(NG)
    return np.cos(angle) * scale, np.sin(angle) * scale


def x_matrix():
    cos, sin = cos_sin(KS)
    eye = np.eye(8)
    return np.concatenate([np.kron(cos, eye), np.kron(sin, eye)], axis=0).astype(bfloat16)


def y_matrix():
    cos, sin = cos_sin(YORDER)
    return np.concatenate([cos, sin], axis=0).astype(bfloat16)


def z_matrix(pairs):
    cos, sin = cos_sin(KS)
    out = np.zeros((NK, 2, pairs, pairs, 2, NG), np.float64)
    for p in range(pairs):
        out[:, 0, p, p, 0] = cos
        out[:, 0, p, p, 1] = sin
        out[:, 1, p, p, 0] = -sin
        out[:, 1, p, p, 1] = cos
    return out.reshape(NK * 2 * pairs, pairs * 2 * NG).astype(bfloat16)


def signed(index):
    return ((index + NG // 2) & (NG - 1)) - NG // 2


def wide_row(ref, which):
    return jnp.concatenate([ref[pl.ds(2 * which, 1), :], ref[pl.ds(2 * which + 1, 1), :]], axis=1)


def density_kernel(
    pairs, dests, col_width,
    v_ref, c_ref, xm_ref, ym_ref, zm_ref, g_ref, ev_ref, ec_ref, ov_ref, oc_ref,
    rho_ref, row_ref,
    first_ref, second_ref, pos_ref, kz_ref, flat_ref,
):
    step = pl.program_id(0)
    lanes = pairs * 2 * NG
    lane = lax.broadcasted_iota(jnp.int32, (1, 1, 2 * NG), 2)
    low = lane < NG
    field_v = v_ref[0].astype(jnp.float32)
    turned = pltpu.roll(field_v, NG, 2)
    v_re = jnp.where(low, field_v, turned)
    v_im = jnp.where(low, turned, -field_v)
    parts = []
    for p in range(pairs):
        field_c = c_ref[p].astype(jnp.float32)
        parts.append(v_re * field_c + v_im * pltpu.roll(field_c, NG, 2))
    sign = jnp.where(lax.broadcasted_iota(jnp.int32, (1, 2 * NG), 1) < NG, 1.0, -1.0)

    def combine(both, rows):
        cols = []
        for p in range(pairs):
            take = slice(p * 2 * NG, (p + 1) * 2 * NG)
            cols.append(both[:rows, take] + sign * pltpu.roll(both[rows : 2 * rows, take], NG, 1))
        return jnp.concatenate(cols, axis=1)

    halves = []
    for half in range(2):
        stacked = jnp.concatenate(
            [
                part[:, half * 8 : half * 8 + 8].reshape(NG * 8, 2 * NG).astype(jnp.bfloat16)
                for part in parts
            ],
            axis=1,
        )
        both = jnp.dot(xm_ref[...], stacked, preferred_element_type=jnp.float32)
        halves.append(combine(both, NK * 8).reshape(NK, 8, lanes))
    merged = jnp.concatenate(halves, axis=1).astype(jnp.bfloat16)
    first_ref[:, pl.ds(pl.multiple_of(step * 16, 16), 16), :] = merged

    @pl.when(step == pl.num_programs(0) - 1)
    def _():
        second_ref[USED_ROWS:, :] = jnp.zeros((ROWS - USED_ROWS, lanes), jnp.float32)
        for i, kx in enumerate(KS):
            both = jnp.dot(ym_ref[...], first_ref[i], preferred_element_type=jnp.float32)
            second_ref[BASE[i] : BASE[i] + rows_for(kx), :] = combine(both, NY)[: rows_for(kx)]
        second = second_ref[...].astype(jnp.bfloat16)
        third = lax.dot_general(
            zm_ref[...], second, (((1,), (1,)), ((), ())), preferred_element_type=jnp.float32
        ).astype(jnp.bfloat16)
        index = g_ref[...]
        comp_x = signed(index >> 12)
        comp_y = signed((index >> 6) & (NG - 1))
        place = 2 * jnp.abs(comp_y) - (comp_y > 0).astype(jnp.int32)
        for i, kx in enumerate(KS):
            place = jnp.where(comp_x == kx, place + BASE[i], place)
        pos_ref[...] = place
        kz_ref[...] = signed(index & (NG - 1)) + KMAX
        row_id = lax.broadcasted_iota(jnp.int32, (ROWS, 256), 0)
        blocks = col_width // 256

        def body(dest, carry):
            for k in range(blocks):
                which = dest * blocks + k
                pos = wide_row(pos_ref, which)
                kz = wide_row(kz_ref, which)
                pick = jnp.where(row_id == pos, 1.0, 0.0).astype(jnp.bfloat16)
                found = jnp.dot(third, pick, preferred_element_type=jnp.float32)
                found = found.reshape(NK, 2 * pairs, 256)
                acc = jnp.zeros((2 * pairs, 256), jnp.float32)
                for i in range(NK):
                    acc = jnp.where(kz == i, found[i], acc)
                for copy in range(2):
                    rho_ref[copy, dest, :, k * 256 : (k + 1) * 256] = acc.astype(jnp.bfloat16)
                flat_ref[which] = acc
            return carry

        lax.fori_loop(0, dests, body, 0)
        which_pair = lax.broadcasted_iota(jnp.int32, (2 * pairs, 128), 0) % pairs
        occ_diff = jnp.zeros((2 * pairs, 128), jnp.float32)
        energy = jnp.ones((2 * pairs, 128), jnp.float32)
        for p in range(pairs):
            occ_diff = jnp.where(which_pair == p, (ov_ref[0] - oc_ref[p]).astype(jnp.float32), occ_diff)
            energy = jnp.where(which_pair == p, ev_ref[0] - ec_ref[p], energy)
        weight = (occ_diff / energy / math.sqrt(1024))[:, :1]

        width = col_width // QUAD

        def weigh(dest, carry):
            wide = jnp.concatenate([flat_ref[dest * blocks + k] for k in range(blocks)], axis=1)
            wide = (wide * weight).astype(jnp.bfloat16).astype(jnp.float32)
            for k in range(QUAD):
                row_ref[dest * QUAD + k] = wide[:, k * width : (k + 1) * width].astype(jnp.bfloat16)
            return carry

        lax.fori_loop(0, dests, weigh, 0)


def densities(valence, conduction, energy_valence, energy_conduction, occ_valence, occ_conduction, gvec_index, n_col):
    pairs = conduction.shape[0]
    lanes = pairs * 2 * NG
    col_width = NPW // n_col
    smem = pl.BlockSpec(memory_space=pltpu.SMEM)
    whole = lambda shape: pl.BlockSpec(shape, lambda s: (0,) * len(shape))
    xm, ym, zm = x_matrix(), y_matrix(), z_matrix(pairs)
    return pl.pallas_call(
        functools.partial(density_kernel, pairs, n_col, col_width),
        grid=(NG // 16,),
        in_specs=[
            pl.BlockSpec((1, NG, 16, 2 * NG), lambda s: (0, 0, s, 0)),
            pl.BlockSpec((pairs, NG, 16, 2 * NG), lambda s: (0, 0, s, 0)),
            whole(xm.shape), whole(ym.shape), whole(zm.shape),
            whole((NPW // 128, 128)),
            smem, smem, smem, smem,
        ],
        out_specs=[
            whole((2, n_col, 2 * pairs, col_width)),
            whole((n_col * QUAD, 2 * pairs, col_width // QUAD)),
        ],
        out_shape=[
            jax.ShapeDtypeStruct((2, n_col, 2 * pairs, col_width), jnp.bfloat16),
            jax.ShapeDtypeStruct((n_col * QUAD, 2 * pairs, col_width // QUAD), jnp.bfloat16),
        ],
        scratch_shapes=[
            pltpu.VMEM((NK, NG, lanes), jnp.bfloat16),
            pltpu.VMEM((ROWS, lanes), jnp.float32),
            pltpu.VMEM((NPW // 128, 128), jnp.int32),
            pltpu.VMEM((NPW // 128, 128), jnp.int32),
            pltpu.VMEM((NPW // 256, 2 * pairs, 256), jnp.float32),
        ],
        compiler_params=pltpu.CompilerParams(vmem_limit_bytes=VMEM_LIMIT),
        cost_estimate=pl.CostEstimate(flops=2 * 10**9, bytes_accessed=6 * 10**6, transcendentals=0),
    )(
        valence, conduction, jnp.asarray(xm), jnp.asarray(ym), jnp.asarray(zm),
        gvec_index.reshape(NPW // 128, 128),
        energy_valence, energy_conduction, occ_valence, occ_conduction,
    )


def spread_kernel(in_ref, after_ref, out_ref):
    core = lax.axis_index("band") % 2
    for j in range(out_ref.shape[1]):
        both = jnp.concatenate(
            [
                in_ref[2 * j + core].astype(jnp.float32),
                in_ref[2 * j + 1 - core].astype(jnp.float32),
            ],
            axis=1,
        ).astype(jnp.bfloat16)
        for dest in range(out_ref.shape[0]):
            out_ref[dest, j] = both


def spread(x, copies, after):
    n_band, po, width = x.shape
    vmem = pl.BlockSpec(memory_space=pltpu.VMEM)
    return pl.pallas_call(
        spread_kernel,
        in_specs=[vmem, pl.BlockSpec(memory_space=pl.ANY)],
        out_specs=vmem,
        out_shape=jax.ShapeDtypeStruct((copies, n_band // 2, po, 2 * width), jnp.bfloat16),
        compiler_params=pltpu.CompilerParams(vmem_limit_bytes=SMALL_LIMIT),
        cost_estimate=pl.CostEstimate(flops=1000, bytes_accessed=1000, transcendentals=0),
    )(x, after)


def left_kernel(in_ref, out_ref, hold_ref):
    band = lax.axis_index("band")
    plane = band // QUAD
    n, blocks, po, double = hold_ref.shape
    duo = 2
    depth = blocks // duo
    width = double // 2
    for v in range(n):
        hold_ref[v] = in_ref[v].astype(jnp.float32)
    turns = [0]
    for step in range(1, depth // 2):
        turns += [step, depth - step]
    turns.append(depth // 2)
    depth_rows = 2 * duo * n * po
    for slot, turn in enumerate(turns):
        source = (plane + depth - turn) % depth
        parts = []
        for high in range(duo):
            f = hold_ref[:, source * duo + high]
            parts += [f[:, :, :width], f[:, :, width:]]
        f = jnp.concatenate(parts, axis=0)
        swapped = jnp.concatenate([f[:, po // 2 :], -f[:, : po // 2]], axis=1)
        for which, src in enumerate((f, swapped)):
            out_ref[which * width : (which + 1) * width, slot * depth_rows : (slot + 1) * depth_rows] = (
                src.reshape(depth_rows, width).astype(jnp.bfloat16).T
            )


def left(rows):
    n, blocks, po, double = rows.shape
    return pl.pallas_call(
        left_kernel,
        out_shape=jax.ShapeDtypeStruct((double, blocks * 2 * n * po), jnp.bfloat16),
        scratch_shapes=[pltpu.VMEM(rows.shape, jnp.float32)],
        compiler_params=pltpu.CompilerParams(vmem_limit_bytes=SMALL_LIMIT),
        cost_estimate=pl.CostEstimate(flops=1000, bytes_accessed=1000, transcendentals=0),
    )(rows)


def product_on(core, turns, l_ref, blocks, out_ref, out_buf, sem):
    double = l_ref.shape[0]
    total = out_ref.shape[-1]
    slots = len(turns)
    quarter = l_ref.shape[1] // slots // QUAD
    copies = []
    for t in range(total // TILE):
        take = slice(t * TILE, (t + 1) * TILE)
        pieces = [None] * (slots * QUAD)
        at = 0
        for step, mirrored, count in turns:
            if step == 0:
                slot = 0
            elif 2 * step == slots:
                slot = slots - 1
            else:
                slot = 2 * step - 1 if core == mirrored else 2 * step
            each = QUAD // count
            for part in range(count):
                for k in range(each):
                    pieces[slot * QUAD + part * each + (k ^ mirrored)] = blocks[at + part][
                        k * quarter : (k + 1) * quarter, take
                    ]
            at += count
        tile = jnp.dot(
            l_ref[...], jnp.concatenate(pieces, axis=0), preferred_element_type=jnp.float32
        )
        out_buf[:, :, take] = tile.reshape(2, double // 2, TILE)
        copy = pltpu.make_async_copy(out_buf.at[:, :, take], out_ref.at[:, :, take], sem.at[t])
        copy.start()
        copies.append(copy)
    for copy in copies:
        copy.wait()


def product_kernel(turns, l_ref, *refs):
    out_ref, out_buf, sem = refs[-3:]
    core = lax.axis_index("band") % 2
    for which in range(2):
        pl.when(core == which)(
            functools.partial(
                product_on, which, turns, l_ref, refs[:-3], out_ref, out_buf, sem
            )
        )


def product(lhs, groups):
    double, all_rows = lhs.shape
    blocks = [b for g in groups for b in g[2]]
    total = blocks[0].shape[1]
    vmem = pl.BlockSpec(memory_space=pltpu.VMEM)
    return pl.pallas_call(
        functools.partial(product_kernel, [g[:2] + (len(g[2]),) for g in groups]),
        in_specs=[vmem] * (1 + len(blocks)),
        out_specs=pl.BlockSpec(memory_space=pl.ANY),
        out_shape=jax.ShapeDtypeStruct((2, double // 2, total), jnp.float32),
        scratch_shapes=[
            pltpu.VMEM((2, double // 2, total), jnp.float32),
            pltpu.SemaphoreType.DMA((total // TILE,)),
        ],
        compiler_params=pltpu.CompilerParams(vmem_limit_bytes=SMALL_LIMIT),
        cost_estimate=pl.CostEstimate(flops=1000, bytes_accessed=1000, transcendentals=0),
    )(lhs, *blocks)


def permute(x, n_band, n_col, move):
    pairs = []
    for band in range(n_band):
        for col in range(n_col):
            to_band, to_col = move(band, col)
            pairs.append((band * n_col + col, to_band * n_col + to_col))
    return lax.ppermute(x, ("band", "col"), pairs)


def local(
    valence, conduction, energy_valence, energy_conduction, occ_valence, occ_conduction, gvec_index
):
    n_col, n_band = lax.axis_size("col"), lax.axis_size("band")
    depth = n_band // QUAD
    send = functools.partial(permute, n_band=n_band, n_col=n_col)
    shift = lambda band, by: (band // QUAD + by) % depth * QUAD + band % QUAD
    ring = lambda x: send(x, move=lambda b, c: (shift(b, 1 if b % 2 == 0 else -1), c))
    swap = lambda x: send(x, move=lambda b, c: (b ^ 1, c))
    rho, weighted = densities(
        valence, conduction, energy_valence, energy_conduction, occ_valence, occ_conduction,
        gvec_index, n_col,
    )
    sheets = [
        [(z * QUAD + high * 2 + core) * n_col + c for high in range(2) for c in range(n_col)]
        for z in range(depth)
        for core in range(2)
    ]
    rho = rho.reshape((2 * n_col,) + rho.shape[2:])
    own = lax.all_to_all(
        rho, ("band", "col"), split_axis=0, concat_axis=0, tiled=True, axis_index_groups=sheets
    )
    size = n_col * own.shape[1]
    own = own.reshape(2 * size, own.shape[2])
    sibling = swap(own)
    near_ring = [jnp.concatenate([own[:size], sibling[:size]], axis=0)]
    near_ring.append(ring(near_ring[0]))
    far_ring = [jnp.concatenate([own[size:], sibling[size:]], axis=0)]
    far_ring.append(ring(far_ring[0]))
    rows = lax.all_to_all(weighted, "band", split_axis=0, concat_axis=0, tiled=True)
    near_ring.append(ring(near_ring[1]))
    far_ring.append(ring(far_ring[1]))
    rows = spread(rows, n_col, near_ring[2])
    rows = lax.all_to_all(rows, "col", split_axis=0, concat_axis=0, tiled=True)
    near_ring.append(ring(near_ring[2]))
    far_ring.append(ring(far_ring[2]))
    last = [ring(near_ring[-1][:size]), ring(far_ring[-1][:size])]
    groups = [(0, 0, (near_ring[0], far_ring[0]))]
    for step in range(1, depth // 2):
        groups.append((step, 0, (near_ring[step], far_ring[step])))
        groups.append((step, 1, (swap(near_ring[step]), swap(far_ring[step]))))
    groups.append((depth // 2, 0, (last[0], swap(last[0]), last[1], swap(last[1]))))
    return product(left(rows), groups)


def solution(mesh):
    return jax.shard_map(
        local,
        mesh=mesh,
        in_specs=(
            P("col", None, None, None),
            P("band", None, None, None),
            P("col"),
            P("band"),
            P("col"),
            P("band"),
            P(),
        ),
        out_specs=P(None, "band", "col"),
        check_vma=False,
    )
```

```python
import functools
import math

import jax
import jax.numpy as jnp
import numpy as np
from jax import lax
from jax.experimental import pallas as pl
from jax.experimental.pallas import tpu as pltpu
from jax.sharding import PartitionSpec as P
from ml_dtypes import bfloat16

NG = 64
NPW = 10240
QUAD = 4
TILE = 256
VMEM_LIMIT = 56 * 1024 * 1024
SMALL_LIMIT = 8 * 1024 * 1024


def sphere_radius():
    axis = (np.arange(NG) + NG // 2) % NG - NG // 2
    square = axis * axis
    length = np.sort((square[:, None, None] + square[None, :, None] + square[None, None, :]).ravel())
    return length[:NPW]


LENGTHS = sphere_radius()
LIMIT = int(LENGTHS[NPW - 1])
KMAX = math.isqrt(LIMIT)
KS = list(range(-KMAX, KMAX + 1))
NK = len(KS)
YORDER = [0]
for step in range(1, KMAX + 1):
    YORDER += [step, -step]
NY = -(-len(YORDER) // 8) * 8
YORDER += [0] * (NY - len(YORDER))


def rows_for(kx):
    return -(-(2 * math.isqrt(LIMIT - kx * kx) + 1) // 8) * 8


BASE = []
total = 0
for kx in KS:
    BASE.append(total)
    total += rows_for(kx)
USED_ROWS = total
ROWS = -(-total // 256) * 256


def cos_sin(freqs):
    product = np.asarray(freqs)[:, None] * np.arange(NG)[None, :] % NG
    angle = (2.0 * math.pi / NG) * product
    scale = 1.0 / math.sqrt(NG)
    return np.cos(angle) * scale, np.sin(angle) * scale


def x_matrix():
    cos, sin = cos_sin(KS)
    eye = np.eye(8)
    return np.concatenate([np.kron(cos, eye), np.kron(sin, eye)], axis=0).astype(bfloat16)


def y_matrix():
    cos, sin = cos_sin(YORDER)
    return np.concatenate([cos, sin], axis=0).astype(bfloat16)


def z_matrix(pairs):
    cos, sin = cos_sin(KS)
    out = np.zeros((NK, 2, pairs, pairs, 2, NG), np.float64)
    for p in range(pairs):
        out[:, 0, p, p, 0] = cos
        out[:, 0, p, p, 1] = sin
        out[:, 1, p, p, 0] = -sin
        out[:, 1, p, p, 1] = cos
    return out.reshape(NK * 2 * pairs, pairs * 2 * NG).astype(bfloat16)


def signed(index):
    return ((index + NG // 2) & (NG - 1)) - NG // 2


def spans(dests, width):
    runs = []
    for dest in range(dests):
        kmax = math.isqrt(int(LENGTHS[(dest + 1) * width - 1]))
        low = BASE[KMAX - kmax]
        high = BASE[KMAX + kmax] + rows_for(kmax)
        size = -(-(high - low) // 128) * 128
        if size < 512:
            size = 512
        if size > 640 or low + size > ROWS:
            low, size = 0, ROWS
        runs.append((low, low + size))
    merged = []
    for dest, run in enumerate(runs):
        if merged and merged[-1][0][1] - merged[-1][0][0] == run[1] - run[0]:
            old = merged[-1]
            wide = run if run[0] <= old[0][0] else old[0]
            merged[-1] = (wide, old[1], dest + 1)
        else:
            merged.append((run, dest, dest + 1))
    return merged


def wide_row(ref, which):
    return jnp.concatenate([ref[pl.ds(2 * which, 1), :], ref[pl.ds(2 * which + 1, 1), :]], axis=1)


def density_kernel(
    pairs, dests, col_width,
    v_ref, c_ref, xm_ref, ym_ref, zm_ref, g_ref, ev_ref, ec_ref, ov_ref, oc_ref,
    rho_ref, row_ref,
    first_ref, second_ref, pos_ref, kz_ref, flat_ref,
):
    step = pl.program_id(0)
    lanes = pairs * 2 * NG
    lane = lax.broadcasted_iota(jnp.int32, (1, 1, 2 * NG), 2)
    low = lane < NG
    field_v = v_ref[0].astype(jnp.float32)
    turned = pltpu.roll(field_v, NG, 2)
    v_re = jnp.where(low, field_v, turned)
    v_im = jnp.where(low, turned, -field_v)
    parts = []
    for p in range(pairs):
        field_c = c_ref[p].astype(jnp.float32)
        parts.append(v_re * field_c + v_im * pltpu.roll(field_c, NG, 2))
    sign = jnp.where(lax.broadcasted_iota(jnp.int32, (1, 2 * NG), 1) < NG, 1.0, -1.0)

    def combine(both, rows):
        cols = []
        for p in range(pairs):
            take = slice(p * 2 * NG, (p + 1) * 2 * NG)
            cols.append(both[:rows, take] + sign * pltpu.roll(both[rows : 2 * rows, take], NG, 1))
        return jnp.concatenate(cols, axis=1)

    halves = []
    for half in range(2):
        stacked = jnp.concatenate(
            [
                part[:, half * 8 : half * 8 + 8].reshape(NG * 8, 2 * NG).astype(jnp.bfloat16)
                for part in parts
            ],
            axis=1,
        )
        both = jnp.dot(xm_ref[...], stacked, preferred_element_type=jnp.float32)
        halves.append(combine(both, NK * 8).reshape(NK, 8, lanes))
    merged = jnp.concatenate(halves, axis=1).astype(jnp.bfloat16)
    first_ref[:, pl.ds(pl.multiple_of(step * 16, 16), 16), :] = merged

    @pl.when(step == pl.num_programs(0) - 1)
    def _():
        second_ref[USED_ROWS:, :] = jnp.zeros((ROWS - USED_ROWS, lanes), jnp.float32)
        for i, kx in enumerate(KS):
            both = jnp.dot(ym_ref[...], first_ref[i], preferred_element_type=jnp.float32)
            second_ref[BASE[i] : BASE[i] + rows_for(kx), :] = combine(both, NY)[: rows_for(kx)]
        second = second_ref[...].astype(jnp.bfloat16)
        third = lax.dot_general(
            zm_ref[...], second, (((1,), (1,)), ((), ())), preferred_element_type=jnp.float32
        ).astype(jnp.bfloat16)
        index = g_ref[...]
        comp_x = signed(index >> 12)
        comp_y = signed((index >> 6) & (NG - 1))
        place = 2 * jnp.abs(comp_y) - (comp_y > 0).astype(jnp.int32)
        for i, kx in enumerate(KS):
            place = jnp.where(comp_x == kx, place + BASE[i], place)
        pos_ref[...] = place
        kz_ref[...] = signed(index & (NG - 1)) + KMAX
        blocks = col_width // 256

        def body(low, table, row_id, dest, carry):
            for k in range(blocks):
                which = dest * blocks + k
                pos = wide_row(pos_ref, which)
                kz = wide_row(kz_ref, which)
                pick = jnp.where(row_id == pos - low, 1.0, 0.0).astype(jnp.bfloat16)
                found = jnp.dot(table, pick, preferred_element_type=jnp.float32)
                found = found.reshape(NK, 2 * pairs, 256)
                acc = jnp.zeros((2 * pairs, 256), jnp.float32)
                for i in range(NK):
                    acc = jnp.where(kz == i, found[i], acc)
                for copy in range(2):
                    rho_ref[copy, dest, :, k * 256 : (k + 1) * 256] = acc.astype(jnp.bfloat16)
                flat_ref[which] = acc
            return carry

        for (low, high), first, end in spans(dests, col_width):
            table = third[:, low:high]
            row_id = lax.broadcasted_iota(jnp.int32, (high - low, 256), 0)
            lax.fori_loop(first, end, functools.partial(body, low, table, row_id), 0)
        which_pair = lax.broadcasted_iota(jnp.int32, (2 * pairs, 128), 0) % pairs
        occ_diff = jnp.zeros((2 * pairs, 128), jnp.float32)
        energy = jnp.ones((2 * pairs, 128), jnp.float32)
        for p in range(pairs):
            occ_diff = jnp.where(which_pair == p, (ov_ref[0] - oc_ref[p]).astype(jnp.float32), occ_diff)
            energy = jnp.where(which_pair == p, ev_ref[0] - ec_ref[p], energy)
        weight = (occ_diff / energy / math.sqrt(1024))[:, :1]

        width = col_width // QUAD

        def weigh(dest, carry):
            wide = jnp.concatenate([flat_ref[dest * blocks + k] for k in range(blocks)], axis=1)
            wide = (wide * weight).astype(jnp.bfloat16).astype(jnp.float32)
            for k in range(QUAD):
                row_ref[dest * QUAD + k] = wide[:, k * width : (k + 1) * width].astype(jnp.bfloat16)
            return carry

        lax.fori_loop(0, dests, weigh, 0)


def densities(valence, conduction, energy_valence, energy_conduction, occ_valence, occ_conduction, gvec_index, n_col):
    pairs = conduction.shape[0]
    lanes = pairs * 2 * NG
    col_width = NPW // n_col
    smem = pl.BlockSpec(memory_space=pltpu.SMEM)
    whole = lambda shape: pl.BlockSpec(shape, lambda s: (0,) * len(shape))
    xm, ym, zm = x_matrix(), y_matrix(), z_matrix(pairs)
    return pl.pallas_call(
        functools.partial(density_kernel, pairs, n_col, col_width),
        grid=(NG // 16,),
        in_specs=[
            pl.BlockSpec((1, NG, 16, 2 * NG), lambda s: (0, 0, s, 0)),
            pl.BlockSpec((pairs, NG, 16, 2 * NG), lambda s: (0, 0, s, 0)),
            whole(xm.shape), whole(ym.shape), whole(zm.shape),
            whole((NPW // 128, 128)),
            smem, smem, smem, smem,
        ],
        out_specs=[
            whole((2, n_col, 2 * pairs, col_width)),
            whole((n_col * QUAD, 2 * pairs, col_width // QUAD)),
        ],
        out_shape=[
            jax.ShapeDtypeStruct((2, n_col, 2 * pairs, col_width), jnp.bfloat16),
            jax.ShapeDtypeStruct((n_col * QUAD, 2 * pairs, col_width // QUAD), jnp.bfloat16),
        ],
        scratch_shapes=[
            pltpu.VMEM((NK, NG, lanes), jnp.bfloat16),
            pltpu.VMEM((ROWS, lanes), jnp.float32),
            pltpu.VMEM((NPW // 128, 128), jnp.int32),
            pltpu.VMEM((NPW // 128, 128), jnp.int32),
            pltpu.VMEM((NPW // 256, 2 * pairs, 256), jnp.float32),
        ],
        compiler_params=pltpu.CompilerParams(vmem_limit_bytes=VMEM_LIMIT),
        cost_estimate=pl.CostEstimate(flops=2 * 10**9, bytes_accessed=6 * 10**6, transcendentals=0),
    )(
        valence, conduction, jnp.asarray(xm), jnp.asarray(ym), jnp.asarray(zm),
        gvec_index.reshape(NPW // 128, 128),
        energy_valence, energy_conduction, occ_valence, occ_conduction,
    )


def spread_kernel(in_ref, after_ref, out_ref):
    core = lax.axis_index("band") % 2
    for j in range(out_ref.shape[1]):
        both = jnp.concatenate(
            [
                in_ref[2 * j + core].astype(jnp.float32),
                in_ref[2 * j + 1 - core].astype(jnp.float32),
            ],
            axis=1,
        ).astype(jnp.bfloat16)
        for dest in range(out_ref.shape[0]):
            out_ref[dest, j] = both


def spread(x, copies, after):
    n_band, po, width = x.shape
    vmem = pl.BlockSpec(memory_space=pltpu.VMEM)
    return pl.pallas_call(
        spread_kernel,
        in_specs=[vmem, pl.BlockSpec(memory_space=pl.ANY)],
        out_specs=vmem,
        out_shape=jax.ShapeDtypeStruct((copies, n_band // 2, po, 2 * width), jnp.bfloat16),
        compiler_params=pltpu.CompilerParams(vmem_limit_bytes=SMALL_LIMIT),
        cost_estimate=pl.CostEstimate(flops=1000, bytes_accessed=1000, transcendentals=0),
    )(x, after)


def left_kernel(in_ref, out_ref, hold_ref):
    band = lax.axis_index("band")
    plane = band // QUAD
    n, blocks, po, double = hold_ref.shape
    duo = 2
    depth = blocks // duo
    width = double // 2
    for v in range(n):
        hold_ref[v] = in_ref[v].astype(jnp.float32)
    turns = [0]
    for step in range(1, depth // 2):
        turns += [step, depth - step]
    turns.append(depth // 2)
    depth_rows = 2 * duo * n * po
    for slot, turn in enumerate(turns):
        source = (plane + depth - turn) % depth
        parts = []
        for high in range(duo):
            f = hold_ref[:, source * duo + high]
            parts += [f[:, :, :width], f[:, :, width:]]
        f = jnp.concatenate(parts, axis=0)
        swapped = jnp.concatenate([f[:, po // 2 :], -f[:, : po // 2]], axis=1)
        for which, src in enumerate((f, swapped)):
            out_ref[which * width : (which + 1) * width, slot * depth_rows : (slot + 1) * depth_rows] = (
                src.reshape(depth_rows, width).astype(jnp.bfloat16).T
            )


def left(rows):
    n, blocks, po, double = rows.shape
    return pl.pallas_call(
        left_kernel,
        out_shape=jax.ShapeDtypeStruct((double, blocks * 2 * n * po), jnp.bfloat16),
        scratch_shapes=[pltpu.VMEM(rows.shape, jnp.float32)],
        compiler_params=pltpu.CompilerParams(vmem_limit_bytes=SMALL_LIMIT),
        cost_estimate=pl.CostEstimate(flops=1000, bytes_accessed=1000, transcendentals=0),
    )(rows)


def product_on(core, turns, l_ref, blocks, out_ref, out_buf, sem):
    double = l_ref.shape[0]
    total = out_ref.shape[-1]
    slots = len(turns)
    quarter = l_ref.shape[1] // slots // QUAD
    copies = []
    for t in range(total // TILE):
        take = slice(t * TILE, (t + 1) * TILE)
        pieces = [None] * (slots * QUAD)
        at = 0
        for step, mirrored, count in turns:
            if step == 0:
                slot = 0
            elif 2 * step == slots:
                slot = slots - 1
            else:
                slot = 2 * step - 1 if core == mirrored else 2 * step
            each = QUAD // count
            for part in range(count):
                for k in range(each):
                    pieces[slot * QUAD + part * each + (k ^ mirrored)] = blocks[at + part][
                        k * quarter : (k + 1) * quarter, take
                    ]
            at += count
        tile = jnp.dot(
            l_ref[...], jnp.concatenate(pieces, axis=0), preferred_element_type=jnp.float32
        )
        out_buf[:, :, take] = tile.reshape(2, double // 2, TILE)
        copy = pltpu.make_async_copy(out_buf.at[:, :, take], out_ref.at[:, :, take], sem.at[t])
        copy.start()
        copies.append(copy)
    for copy in copies:
        copy.wait()


def product_kernel(turns, l_ref, *refs):
    out_ref, out_buf, sem = refs[-3:]
    core = lax.axis_index("band") % 2
    for which in range(2):
        pl.when(core == which)(
            functools.partial(
                product_on, which, turns, l_ref, refs[:-3], out_ref, out_buf, sem
            )
        )


def product(lhs, groups):
    double, all_rows = lhs.shape
    blocks = [b for g in groups for b in g[2]]
    total = blocks[0].shape[1]
    vmem = pl.BlockSpec(memory_space=pltpu.VMEM)
    return pl.pallas_call(
        functools.partial(product_kernel, [g[:2] + (len(g[2]),) for g in groups]),
        in_specs=[vmem] * (1 + len(blocks)),
        out_specs=pl.BlockSpec(memory_space=pl.ANY),
        out_shape=jax.ShapeDtypeStruct((2, double // 2, total), jnp.float32),
        scratch_shapes=[
            pltpu.VMEM((2, double // 2, total), jnp.float32),
            pltpu.SemaphoreType.DMA((total // TILE,)),
        ],
        compiler_params=pltpu.CompilerParams(vmem_limit_bytes=SMALL_LIMIT),
        cost_estimate=pl.CostEstimate(flops=1000, bytes_accessed=1000, transcendentals=0),
    )(lhs, *blocks)


def permute(x, n_band, n_col, move):
    pairs = []
    for band in range(n_band):
        for col in range(n_col):
            to_band, to_col = move(band, col)
            pairs.append((band * n_col + col, to_band * n_col + to_col))
    return lax.ppermute(x, ("band", "col"), pairs)


def local(
    valence, conduction, energy_valence, energy_conduction, occ_valence, occ_conduction, gvec_index
):
    n_col, n_band = lax.axis_size("col"), lax.axis_size("band")
    depth = n_band // QUAD
    send = functools.partial(permute, n_band=n_band, n_col=n_col)
    shift = lambda band, by: (band // QUAD + by) % depth * QUAD + band % QUAD
    ring = lambda x: send(x, move=lambda b, c: (shift(b, 1 if b % 2 == 0 else -1), c))
    swap = lambda x: send(x, move=lambda b, c: (b ^ 1, c))
    rho, weighted = densities(
        valence, conduction, energy_valence, energy_conduction, occ_valence, occ_conduction,
        gvec_index, n_col,
    )
    sheets = [
        [(z * QUAD + high * 2 + core) * n_col + c for high in range(2) for c in range(n_col)]
        for z in range(depth)
        for core in range(2)
    ]
    rho = rho.reshape((2 * n_col,) + rho.shape[2:])
    own = lax.all_to_all(
        rho, ("band", "col"), split_axis=0, concat_axis=0, tiled=True, axis_index_groups=sheets
    )
    size = n_col * own.shape[1]
    own = own.reshape(2 * size, own.shape[2])
    sibling = swap(own)
    near_ring = [jnp.concatenate([own[:size], sibling[:size]], axis=0)]
    near_ring.append(ring(near_ring[0]))
    far_ring = [jnp.concatenate([own[size:], sibling[size:]], axis=0)]
    far_ring.append(ring(far_ring[0]))
    rows = lax.all_to_all(weighted, "band", split_axis=0, concat_axis=0, tiled=True)
    near_ring.append(ring(near_ring[1]))
    far_ring.append(ring(far_ring[1]))
    rows = spread(rows, n_col, near_ring[2])
    rows = lax.all_to_all(rows, "col", split_axis=0, concat_axis=0, tiled=True)
    near_ring.append(ring(near_ring[2]))
    far_ring.append(ring(far_ring[2]))
    last = [ring(near_ring[-1][:size]), ring(far_ring[-1][:size])]
    groups = [(0, 0, (near_ring[0], far_ring[0]))]
    for step in range(1, depth // 2):
        groups.append((step, 0, (near_ring[step], far_ring[step])))
        groups.append((step, 1, (swap(near_ring[step]), swap(far_ring[step]))))
    groups.append((depth // 2, 0, (last[0], swap(last[0]), last[1], swap(last[1]))))
    return product(left(rows), groups)


def solution(mesh):
    return jax.shard_map(
        local,
        mesh=mesh,
        in_specs=(
            P("col", None, None, None),
            P("band", None, None, None),
            P("col"),
            P("band"),
            P("col"),
            P("band"),
            P(),
        ),
        out_specs=P(None, "band", "col"),
        check_vma=False,
    )
```
